32 devices in a mesh: row: 8 (over y, x, core), col: 4 (over z).
Axes of the slice: x: 2, y: 2, z: 4, core: 2. Of those that a mesh axis runs over, the one named last changes fastest.
Arguments:
- laplacian: bfloat16 [8192, 8192], P('row', 'col')
- interp: bfloat16 [8192, 128], P('row'), may hold values from -0.375 to 0.375
- vectors: bfloat16 [32, 8192], P(None, 'row'), may hold values from -6 to 6
- pairs: int32 [32, 2], replicated, may hold values from 0 to 63, as said below
Outputs:
- coarse: bfloat16 [4096, 4096], P(('row', 'col'))
- coarse_vectors: bfloat16 [32, 4096], P(None, 'row')
The draws below stay inside these ranges and needn't reach their ends.
Inputs may be any that keep to these rules, and one draw needn't show every extreme that they name: Row c holds (a, b), where a lies among the 8 fine tile rows of row index g = (c // 4) mod 4, that is a // 8 == g, and b // 8 == g + 4. Every fine tile row appears exactly once in pairs.
All inputs are finite; a program needn't handle non-finite values.
Results may differ from the reference program's by a relative error of at most 0.0058.
Values may be sent and summed in bfloat16 or wider, within the bound.
No kernel may reach another device: no remote copies, remote signals or barrier semaphores. Data moves between devices by JAX's collectives and lax.ppermute only.
A program may use at most 64 MiB of HBM per device.

```python
import jax
import jax.numpy as jnp
from jax import lax

B = 128
K = 32
TR = 8
NT = 64
NV = 8192
NC = 32
GROUPS = 4


def draw_laplacian(key, part):
    vertex_count = NT * B
    first_key = jax.random.fold_in(key, 0)
    base_draw = jax.random.normal(first_key, (vertex_count, vertex_count), jnp.float32)
    symmetric = (base_draw + base_draw.T) * 0.7071
    identity = jnp.eye(vertex_count, dtype=jnp.float32)
    return (symmetric + 3.0 * identity).astype(jnp.bfloat16)


def draw_pairs(key, part):
    half_rows = TR // 2
    all_keys = jax.random.split(key, 2 * GROUPS)
    matching = jax.vmap(lambda sub_key: jax.random.permutation(sub_key, TR))(all_keys[:GROUPS]).astype(jnp.int32)
    ordering = jax.vmap(lambda sub_key: jax.random.permutation(sub_key, TR))(all_keys[GROUPS:]).astype(jnp.int32)
    group_ids = jnp.arange(GROUPS, dtype=jnp.int32)[:, None]
    low_rows = group_ids * TR + ordering
    high_rows = (group_ids + GROUPS) * TR + jnp.take_along_axis(matching, ordering, axis=1)
    stacked = jnp.stack([low_rows, high_rows], axis=-1)
    front_half = stacked[:, :half_rows].reshape(GROUPS * half_rows, 2)
    back_half = stacked[:, half_rows:].reshape(GROUPS * half_rows, 2)
    return jnp.concatenate([front_half, back_half], axis=0).astype(jnp.int32)


def steps_of(own_key, extent, shards, low, high):
    level = 1.0
    for position, shards_of in shards:
        draws = jax.random.uniform(jax.random.fold_in(jax.random.fold_in(own_key, 6), position), (shards_of,), jnp.float32, low / len(shards), high / len(shards))
        level = level * jnp.repeat(jnp.exp(draws), extent[position] // shards_of).reshape((-1,) + (1,) * (len(extent) - 1 - position))
    return level


def gaussian(rng, dims, width, reach, pieces=(), kind=jnp.bfloat16):
    values = jax.random.normal(rng, dims, jnp.float32) * width
    if len(pieces) > 0:
        values = steps_of(rng, dims, pieces, -0.22, 0.18) * values
    return jnp.clip(values, min=-reach, max=reach).astype(kind)


def setup_inputs(seed: int = 0) -> dict:
    key_of = jax.random.split(jax.random.key(seed), 5)
    laplacian = draw_laplacian(jax.random.fold_in(key_of[4], 71), 0)
    interp = gaussian(key_of[1], (NV, B), (2 * B) ** -0.5, 0.375, ((0, 8),))
    vectors = gaussian(key_of[2], (K, NV), 1.0, 6.0, ((1, 8),))
    pairs = draw_pairs(jax.random.fold_in(key_of[4], 71), 0)
    return {"laplacian": laplacian, "interp": interp, "vectors": vectors, "pairs": pairs}


def reference(laplacian, interp, vectors, pairs):
    fine_tiles = laplacian.reshape(NT, B, NT, B)
    interp_blocks = interp.reshape(NT, B, B).astype(jnp.float32)

    def project_row(operands):
        row_tiles, left_block = operands
        product = jnp.einsum('xjy,jyb->xjb', row_tiles.astype(jnp.float32), interp_blocks).astype(jnp.bfloat16)
        return jnp.einsum('xa,xjb->ajb', left_block, product.astype(jnp.float32)).astype(jnp.bfloat16)

    projected = lax.map(project_row, (fine_tiles, interp_blocks))
    low_member = pairs[:, 0].astype(jnp.int32)
    high_member = pairs[:, 1].astype(jnp.int32)
    row_sum = jnp.take(projected, low_member, axis=0).astype(jnp.float32) + jnp.take(projected, high_member, axis=0).astype(jnp.float32)
    coarse = jnp.take(row_sum, low_member, axis=2) + jnp.take(row_sum, high_member, axis=2)
    coarse = coarse.astype(jnp.bfloat16).reshape(NC * B, NC * B)
    restricted = jnp.einsum('kix,ixa->kia', vectors.reshape(K, NT, B).astype(jnp.float32), interp_blocks).astype(jnp.bfloat16)
    coarse_vectors = jnp.take(restricted, low_member, axis=1).astype(jnp.float32) + jnp.take(restricted, high_member, axis=1).astype(jnp.float32)
    coarse_vectors = coarse_vectors.astype(jnp.bfloat16).reshape(K, NC * B)
    return coarse, coarse_vectors
```

```python
import functools

import jax
import jax.numpy as jnp
from jax import lax
from jax.experimental import pallas as pl
from jax.experimental.pallas import tpu as pltpu
from jax.sharding import PartitionSpec as P


def contract_rows(left, right):
    return lax.dot_general(
        left, right, (((0,), (0,)), ((), ())), preferred_element_type=jnp.float32
    )


def exchange(block, axis, flip):
    count = lax.axis_size(axis)
    return lax.ppermute(block, axis, [(i, i ^ flip) for i in range(count)])


def row_of(place, pairs, coarse_row, fine_rows, upper):
    return pairs[coarse_row, upper] - place[0] * fine_rows


def project(laplacian, interp, pairs, place, received, step, mine, width):
    tile = interp.shape[1]
    fine_rows = interp.shape[0] // tile
    coarse_rows = fine_rows // 2
    cols = laplacian.shape[1]
    half = lax.axis_size("row") // 2
    count = coarse_rows * tile // lax.axis_size("col")
    flip = 0 if mine else half

    def row_tile(pairs_ref, place_ref):
        row, col = place_ref[0], place_ref[1]
        coarse_row = (row ^ flip) * coarse_rows + (col ^ step) * count // tile
        return pairs_ref[coarse_row * 2 + row // half] - row * fine_rows

    def body(pairs_ref, place_ref, interp_ref, lap_ref, *refs):
        out_ref = refs[-1] if count == tile else refs[-2]
        result = contract_rows(interp_ref[...], lap_ref[...])
        if count != tile:
            whole_ref = refs[-1]
            whole_ref[...] = result
            begin = ((place_ref[1] ^ step) * count) % tile
            result = whole_ref[pl.ds(pl.multiple_of(begin, count), count), :]
        if received is not None:
            result = result + refs[0][...].astype(jnp.float32)
        out_ref[...] = result.astype(out_ref.dtype)

    in_specs = [
        pl.BlockSpec((tile, tile), lambda n, pr, pc: (row_tile(pr, pc), 0)),
        pl.BlockSpec((tile, width), lambda n, pr, pc: (row_tile(pr, pc), n)),
    ]
    operands = [interp, laplacian]
    if received is not None:
        in_specs.append(pl.BlockSpec((count, width), lambda n, pr, pc: (0, n)))
        operands.append(received)
    return pl.pallas_call(
        body,
        out_shape=jax.ShapeDtypeStruct((count, cols), jnp.bfloat16),
        grid_spec=pltpu.PrefetchScalarGridSpec(
            num_scalar_prefetch=2,
            grid=(cols // width,),
            in_specs=in_specs,
            out_specs=pl.BlockSpec((count, width), lambda n, pr, pc: (0, n)),
            scratch_shapes=[] if count == tile else [pltpu.VMEM((tile, width), jnp.float32)],
        ),
        cost_estimate=pl.CostEstimate(
            flops=2 * tile * tile * cols, bytes_accessed=6 * tile * cols, transcendentals=0
        ),
        name="project_mine" if mine else "project_partner",
    )(pairs, place, *operands)


def finish(near, far, every_interp, pairs, place, before, step, fine_cols):
    tile = every_interp.shape[1]
    count = near.shape[0]
    half = lax.axis_size("col") // 2
    coarse_cols = fine_cols // 2
    total = every_interp.shape[0] // 2

    def body(pairs_ref, place_ref, near_ref, far_ref, interp_ref, *refs):
        out_ref = refs[-1]
        col = place_ref[1]
        upper = col // half
        first = (pl.program_id(0) * half + (col ^ step) % half) * coarse_cols
        for k in range(coarse_cols):
            near_tile = pairs_ref[(first + k) * 2 + upper]
            far_tile = pairs_ref[(first + k) * 2 + 1 - upper]
            result = None
            for ref, j, owner in (
                (near_ref, near_tile, col ^ step),
                (far_ref, far_tile, col ^ step ^ half),
            ):
                start = pl.multiple_of((j - owner * fine_cols) * tile, tile)
                rows = pl.multiple_of(j * tile, tile)
                part = jnp.dot(
                    ref[:, pl.ds(start, tile)],
                    interp_ref[pl.ds(rows, tile), :],
                    preferred_element_type=jnp.float32,
                )
                result = part if result is None else result + part
            out_ref[:, k * tile : (k + 1) * tile] = result.astype(out_ref.dtype)

    whole = pl.BlockSpec(near.shape, lambda n, pr, pc: (0, 0))
    in_specs = [whole, whole, pl.BlockSpec(every_interp.shape, lambda n, pr, pc: (0, 0))]
    operands = [near, far, every_interp]
    aliases = {}
    if before is not None:
        in_specs.append(pl.BlockSpec(memory_space=pl.ANY))
        operands.append(before)
        aliases = {5: 0}
    return pl.pallas_call(
        body,
        out_shape=jax.ShapeDtypeStruct((count, total), jnp.bfloat16),
        grid_spec=pltpu.PrefetchScalarGridSpec(
            num_scalar_prefetch=2,
            grid=(2,),
            in_specs=in_specs,
            out_specs=pl.BlockSpec(
                (count, coarse_cols * tile),
                lambda n, pr, pc: (0, n * half + (pc[1] ^ step) % half),
            ),
        ),
        input_output_aliases=aliases,
        cost_estimate=pl.CostEstimate(
            flops=4 * count * tile * 2 * coarse_cols * tile,
            bytes_accessed=2 * every_interp.size,
            transcendentals=0,
        ),
        compiler_params=pltpu.CompilerParams(vmem_limit_bytes=40 * 1024 * 1024),
        name="finish",
    )(pairs, place, *operands)


def restrict(vectors, interp, pairs, place):
    tile = interp.shape[1]
    fine_rows = interp.shape[0] // tile
    coarse_rows = fine_rows // 2
    half = lax.axis_size("row") // 2

    def body(pairs_ref, place_ref, vec_ref, interp_ref, keep_ref, send_ref):
        row = place_ref[0]
        for out_ref, flip in ((keep_ref, 0), (send_ref, half)):
            for k in range(coarse_rows):
                i = pairs_ref[((row ^ flip) * coarse_rows + k) * 2 + row // half] - row * fine_rows
                at = pl.ds(pl.multiple_of(i * tile, tile), tile)
                out_ref[:, k * tile : (k + 1) * tile] = jnp.dot(
                    vec_ref[:, at], interp_ref[at, :], preferred_element_type=jnp.float32
                ).astype(out_ref.dtype)

    shape = jax.ShapeDtypeStruct((vectors.shape[0], coarse_rows * tile), jnp.bfloat16)
    return pl.pallas_call(
        body,
        out_shape=(shape, shape),
        in_specs=[
            pl.BlockSpec(memory_space=pltpu.SMEM),
            pl.BlockSpec(memory_space=pltpu.SMEM),
            pl.BlockSpec(memory_space=pltpu.VMEM),
            pl.BlockSpec(memory_space=pltpu.VMEM),
        ],
        out_specs=(pl.BlockSpec(memory_space=pltpu.VMEM),) * 2,
        name="restrict",
    )(pairs, place, vectors, interp)


def on_device(laplacian, interp, vectors, pairs):
    tile = interp.shape[1]
    fine_cols = laplacian.shape[1] // tile
    row_half = lax.axis_size("row") // 2
    col_count = lax.axis_size("col")
    col_half = col_count // 2
    width = min(512, laplacian.shape[1])
    place = jnp.stack([lax.axis_index("row"), lax.axis_index("col")]).astype(jnp.int32)
    pairs = pairs.reshape(-1)

    steps = list(range(col_half, col_count)) + list(range(col_half - 1, -1, -1))
    away = {}
    for step in steps:
        block = project(laplacian, interp, pairs, place, None, step, False, width)
        away[step] = exchange(block, "row", row_half)
    every_interp = lax.all_gather(interp, "row", axis=0, tiled=True)
    keep, send = restrict(vectors, interp, pairs, place)
    far_vec = exchange(send, "row", row_half)
    held = {}
    for step in steps:
        block = project(laplacian, interp, pairs, place, away[step], step, True, width)
        held[step] = exchange(block, "col", step) if step else block
    coarse_vectors = (keep.astype(jnp.float32) + far_vec.astype(jnp.float32)).astype(jnp.bfloat16)
    coarse = None
    for step in range(col_half):
        coarse = finish(
            held[step], held[step ^ col_half], every_interp, pairs, place, coarse, step, fine_cols
        )
    return (coarse, coarse_vectors)


def solution(mesh):
    placed = (P("row", "col"), P("row", None), P(None, "row"), P())
    return jax.shard_map(
        on_device,
        mesh=mesh,
        in_specs=placed,
        out_specs=(P(("row", "col"), None), P(None, "row")),
        check_vma=False,
    )
```

```python
import jax
import jax.numpy as jnp
from jax import lax
from jax.experimental import pallas as pl
from jax.experimental.pallas import tpu as pltpu
from jax.sharding import PartitionSpec as P


AHEAD = 2
HEAD = 1
GATHER = 1
VECTORS = 2
VECTORS_AT = '0a'
ZAFTER = {}
FINISH = 1000000000
JOBS = 2
WAITS = {'1a': ['z2a'], '0a': ['z3a', 'g2']}


def CHUNKS(half, count):
    chunks = [(half, 0, 8), (half, 8, 16)]
    for far, near in zip(range(half + 1, count), range(1, half)):
        chunks += [(far, 0, 16), (near, 0, 16)]
    return chunks + [(0, 0, 16)]


def estimate(flops=1000):
    return pl.CostEstimate(flops=flops, bytes_accessed=flops // 1000, transcendentals=0)


def in_hbm(value):
    return pltpu.with_memory_space_constraint(value, pltpu.HBM)


def contract_rows(left, right):
    return lax.dot_general(
        left, right, (((0,), (0,)), ((), ())), preferred_element_type=jnp.float32
    )


def exchange(block, axis, flip, name="p"):
    count = lax.axis_size(axis)
    with jax.named_scope(name):
        return lax.ppermute(block, axis, [(i, i ^ flip) for i in range(count)])
    return lax.ppermute(block, axis, [(i, i ^ flip) for i in range(count)])


def after(value, *earlier):
    return lax.optimization_barrier((value, *earlier))[0]


def project(laplacian, interp, pairs, jobs, *earlier, flops=1000):
    tile = interp.shape[1]
    fine_rows = interp.shape[0] // tile
    coarse_rows = fine_rows // 2
    cols = laplacian.shape[1]
    half = lax.axis_size("row") // 2
    count = coarse_rows * tile // lax.axis_size("col")
    outs = [
        jax.ShapeDtypeStruct((count, end - begin), dtype)
        for _, _, dtype, spans in jobs
        for begin, end in spans
    ]

    def body(pairs_ref, interp_ref, lap_ref, *refs):
        out_refs = list(refs[len(earlier) : len(earlier) + len(outs)])
        lap_buf, interp_buf, whole_ref, sems = refs[len(earlier) + len(outs) :]
        row, col = lax.axis_index("row"), lax.axis_index("col")
        copies = []
        for slot, (step, mine, _, _) in enumerate(jobs):
            owner = row if mine else row ^ half
            coarse_row = owner * coarse_rows + (col ^ step) * count // tile
            local = pairs_ref[row // half, coarse_row] - row * fine_rows
            at = pl.ds(pl.multiple_of(local * tile, tile), tile)
            for which, (ref, buf) in enumerate(((interp_ref, interp_buf), (lap_ref, lap_buf))):
                copy = pltpu.make_async_copy(ref.at[at, :], buf.at[slot], sems.at[which, slot])
                copy.start()
                copies.append(copy)
        for slot, (step, mine, _, spans) in enumerate(jobs):
            copies[2 * slot].wait()
            copies[2 * slot + 1].wait()
            left = interp_buf[slot]
            for begin, end in spans:
                out_ref = out_refs.pop(0)
                result = contract_rows(left, lap_buf[slot, :, begin:end])
                if count != tile:
                    whole_ref[:, : end - begin] = result
                    first = pl.multiple_of(((col ^ step) * count) % tile, count)
                    result = whole_ref[pl.ds(first, count), : end - begin]
                out_ref[...] = result.astype(out_ref.dtype)

    spare = (8, 128) if count == tile else (tile, cols)
    size = sum(out.size * out.dtype.itemsize for out in outs)
    size += len(jobs) * tile * (cols + tile) * 2 + spare[0] * spare[1] * 4
    return pl.pallas_call(
        body,
        out_shape=outs,
        in_specs=[pl.BlockSpec(memory_space=pltpu.SMEM)]
        + [pl.BlockSpec(memory_space=pl.ANY)] * (2 + len(earlier)),
        out_specs=[pl.BlockSpec(memory_space=pltpu.VMEM)] * len(outs),
        scratch_shapes=[
            pltpu.VMEM((len(jobs), tile, cols), jnp.bfloat16),
            pltpu.VMEM((len(jobs), tile, tile), jnp.bfloat16),
            pltpu.VMEM(spare, jnp.float32),
            pltpu.SemaphoreType.DMA((2, len(jobs))),
        ],
        compiler_params=pltpu.CompilerParams(vmem_limit_bytes=size + 4 * 1024 * 1024),
        cost_estimate=estimate(flops),
        name="project",
    )(in_hbm(pairs), in_hbm(interp), in_hbm(laplacian), *earlier)


def combine(own, begin, received, *earlier):
    end = begin + received.shape[1]

    def body(own_ref, received_ref, *refs):
        total = own_ref[:, begin:end].astype(jnp.float32) + received_ref[...].astype(jnp.float32)
        refs[-1][...] = total.astype(refs[-1].dtype)

    return pl.pallas_call(
        body,
        out_shape=jax.ShapeDtypeStruct(received.shape, jnp.bfloat16),
        in_specs=[pl.BlockSpec(memory_space=pltpu.VMEM)] * 2
        + [pl.BlockSpec(memory_space=pl.ANY)] * len(earlier),
        out_specs=pl.BlockSpec(memory_space=pltpu.VMEM),
        compiler_params=pltpu.CompilerParams(vmem_limit_bytes=8 * 1024 * 1024),
        cost_estimate=estimate(),
        name="combine",
    )(own, received, *earlier)


def gather_blocks(block, axis):
    blocks, flip = [block], lax.axis_size(axis) // 2
    while flip:
        blocks += [exchange(part, axis, flip, f"gather{flip}") for part in blocks]
        flip //= 2
    return blocks


def finish(jobs, interp_blocks, pairs, before, fine_cols, *earlier):
    tile = interp_blocks[0].shape[1]
    fine_rows = interp_blocks[0].shape[0] // tile
    count = jobs[0][0][0].shape[0]
    row_count = lax.axis_size("row")
    half = lax.axis_size("col") // 2
    coarse_cols = fine_cols // 2
    width = coarse_cols * tile
    total = row_count * fine_rows * tile // 2
    pieces = [
        (2 * n + which, part)
        for n, (near, far, _) in enumerate(jobs)
        for which, parts in enumerate((near, far))
        for part in parts
    ]
    sources = [*interp_blocks, *(part for _, part in pieces)]

    def body(pairs_ref, *refs):
        out_ref, wide, interp_buf, buf, sem, fetch = refs[-6:]
        row, col = lax.axis_index("row"), lax.axis_index("col")
        upper = col // half
        begins, fetches = [0] * (2 * len(jobs)), []
        for k, ref in enumerate(refs[: len(sources)]):
            if k < len(interp_blocks):
                target = interp_buf.at[k]
            else:
                which = pieces[k - len(interp_blocks)][0]
                begin = begins[which]
                begins[which] = begin + ref.shape[1]
                target = wide.at[which, :, begin : begins[which]]
            fetches.append(pltpu.make_async_copy(ref, target, fetch.at[k]))
        for copy in fetches:
            copy.start()
        for copy in fetches:
            copy.wait()
        copies = []
        for n, (_, _, step) in enumerate(jobs):
            for part in range(2):
                group = part * half + (col ^ step) % half
                for k in range(coarse_cols):
                    d = group * coarse_cols + k
                    result = None
                    for which, j, owner in (
                        (0, pairs_ref[upper, d], col ^ step),
                        (1, pairs_ref[1 - upper, d], col ^ step ^ half),
                    ):
                        start = pl.multiple_of((j - owner * fine_cols) * tile, tile)
                        source = (j // fine_rows) ^ row
                        place, bit = 0, row_count // 2
                        while bit:
                            place = place * 2 + source % 2
                            source, bit = source // 2, bit // 2
                        at = pl.multiple_of((j % fine_rows) * tile, tile)
                        product = jnp.dot(
                            wide[2 * n + which, :, pl.ds(start, tile)],
                            interp_buf[place, pl.ds(at, tile), :],
                            preferred_element_type=jnp.float32,
                        )
                        result = product if result is None else result + product
                    buf[2 * n + part, :, k * tile : (k + 1) * tile] = result.astype(buf.dtype)
                copy = pltpu.make_async_copy(
                    buf.at[2 * n + part],
                    out_ref.at[:, pl.ds(pl.multiple_of(group * width, width), width)],
                    sem.at[2 * n + part],
                )
                copy.start()
                copies.append(copy)
        for copy in copies:
            copy.wait()

    operands = [pairs, *sources]
    aliases = {}
    if before is not None:
        aliases = {len(operands): 0}
        operands.append(before)
    operands += earlier
    blocks = len(interp_blocks)
    size = blocks * fine_rows * tile * tile * 2 + 2 * len(jobs) * count * (fine_cols * tile + width) * 2
    return pl.pallas_call(
        body,
        out_shape=jax.ShapeDtypeStruct((count, total), jnp.bfloat16),
        in_specs=[pl.BlockSpec(memory_space=pltpu.SMEM)]
        + [pl.BlockSpec(memory_space=pl.ANY)] * (len(operands) - 1),
        out_specs=pl.BlockSpec(memory_space=pl.ANY),
        scratch_shapes=[
            pltpu.VMEM((2 * len(jobs), count, fine_cols * tile), jnp.bfloat16),
            pltpu.VMEM((blocks, fine_rows * tile, tile), jnp.bfloat16),
            pltpu.VMEM((2 * len(jobs), count, width), jnp.bfloat16),
            pltpu.SemaphoreType.DMA((2 * len(jobs),)),
            pltpu.SemaphoreType.DMA((len(sources),)),
        ],
        input_output_aliases=aliases,
        cost_estimate=estimate(FINISH),
        compiler_params=pltpu.CompilerParams(vmem_limit_bytes=size + 4 * 1024 * 1024),
        name="finish",
    )(*operands)


def restrict(vectors, interp, pairs, *earlier):
    tile = interp.shape[1]
    fine_rows = interp.shape[0] // tile
    coarse_rows = fine_rows // 2
    half = lax.axis_size("row") // 2

    def body(pairs_ref, vec_ref, interp_ref, *refs):
        keep_ref, send_ref = refs[-2:]
        row = lax.axis_index("row")
        for out_ref, flip in ((keep_ref, 0), (send_ref, half)):
            for k in range(coarse_rows):
                i = pairs_ref[row // half, (row ^ flip) * coarse_rows + k] - row * fine_rows
                at = pl.ds(pl.multiple_of(i * tile, tile), tile)
                out_ref[:, k * tile : (k + 1) * tile] = jnp.dot(
                    vec_ref[:, at], interp_ref[at, :], preferred_element_type=jnp.float32
                ).astype(out_ref.dtype)

    shape = jax.ShapeDtypeStruct((vectors.shape[0], coarse_rows * tile), jnp.bfloat16)
    return pl.pallas_call(
        body,
        out_shape=(shape, shape),
        in_specs=[
            pl.BlockSpec(memory_space=pltpu.SMEM),
            pl.BlockSpec(memory_space=pltpu.VMEM),
            pl.BlockSpec(memory_space=pltpu.VMEM),
        ]
        + [pl.BlockSpec(memory_space=pl.ANY)] * len(earlier),
        out_specs=(pl.BlockSpec(memory_space=pltpu.VMEM),) * 2,
        compiler_params=pltpu.CompilerParams(vmem_limit_bytes=4 * 1024 * 1024),
        cost_estimate=estimate(),
        name="restrict",
    )(pairs, vectors, interp, *earlier)


def on_device(laplacian, interp, vectors, pairs):
    tile = interp.shape[1]
    cols = laplacian.shape[1]
    fine_rows, fine_cols = interp.shape[0] // tile, cols // tile
    row_half = lax.axis_size("row") // 2
    col_count = lax.axis_size("col")
    col_half = col_count // 2
    pairs = pairs.T

    whole = [(0, cols)]
    order = CHUNKS(col_half, col_count)
    steps = list(dict.fromkeys(step for step, _, _ in order))
    spans = {
        step: [(lo * cols // 16, hi * cols // 16) for other, lo, hi in order if other == step]
        for step in steps
    }
    labels = [f"{step}{'abcdefgh'[spans[step].index((lo * cols // 16, hi * cols // 16))]}" for step, lo, hi in order]
    head = HEAD
    cut = sum(len(spans[step]) for step in steps[:head])
    sent = project(
        laplacian, interp, pairs, [(s, False, jnp.bfloat16, spans[s]) for s in steps[:head]]
    )
    sent += project(
        laplacian, interp, pairs, [(s, False, jnp.bfloat16, spans[s]) for s in steps[head:]], sent[0]
    )
    grouped = [(step, span) for step in steps for span in spans[step]]
    sent = dict(zip(grouped, sent))
    kept = project(
        laplacian, interp, pairs, [(s, True, jnp.float32, whole) for s in steps], sent[grouped[cut]]
    )
    kept = dict(zip(steps, kept))
    named, totals, held = {}, [kept[0]], {step: [] for step in steps}
    for k, (step, lo, hi) in enumerate(order):
        name, span = labels[k], (lo * cols // 16, hi * cols // 16)
        block = sent[step, span]
        if k >= AHEAD:
            block = after(block, totals[k + 1 - AHEAD])
        block = exchange(block, "row", row_half, "y" + name)
        waits = totals[-1:] + [named[w] for w in WAITS.get(name, ()) if w in named]
        if name == VECTORS_AT:
            coarse_vectors = combine(keep, 0, far_vec, totals[-1])
            waits.append(coarse_vectors)
        total = combine(kept[step], span[0], block, *waits)
        totals.append(total)
        if step:
            later = [named[w] for w in ZAFTER.get(name, ()) if w in named]
            total = exchange(after(total, *later) if later else total, "col", step, "z" + name)
        named["z" + name] = total
        held[step].append(total)
        if k == GATHER:
            interp_blocks = gather_blocks(after(interp, totals[-1]), "row")
            for place, value in enumerate(interp_blocks):
                named[f"g{place}"] = value
        if k == VECTORS:
            keep, send = restrict(vectors, interp, pairs, totals[-1])
            named["v"] = far_vec = exchange(send, "row", row_half, "vectors")
    if not VECTORS_AT:
        coarse_vectors = combine(keep, 0, far_vec, totals[-1])
    coarse = None
    jobs = [(held[step], held[step ^ col_half], step) for step in range(col_half)]
    for k in range(0, len(jobs), JOBS):
        coarse = finish(jobs[k : k + JOBS], interp_blocks, pairs, coarse, fine_cols)
    return (coarse, coarse_vectors)


def solution(mesh):
    placed = (P("row", "col"), P("row", None), P(None, "row"), P())
    return jax.shard_map(
        on_device,
        mesh=mesh,
        in_specs=placed,
        out_specs=(P(("row", "col"), None), P(None, "row")),
        check_vma=False,
    )
```

```python
import jax
import jax.numpy as jnp
from jax import lax
from jax.experimental import pallas as pl
from jax.experimental.pallas import tpu as pltpu
from jax.sharding import PartitionSpec as P


YAFTER = {'3a': ['2a'], '1a': ['2b'], '1b': ['3a'], '3b': ['1a'], '0a': ['1b'], '0b': ['3b']}
HEAD = 1
GATHER = '2b'
VECTORS = '1b'
VECTORS_AT = ''
ZAFTER = {}
FINISH = 1000
JOBS = 2
ASSEMBLE_Y = ''
VECTORS_Y = ''
PFLOPS = (1000, 1000)
CFLOPS = 1000
ASSEMBLE_AT = ''
VECFLOPS = 1000
VECDEP = -1
ASSEMBLE = 100000000
WAITS = {'3a': ['z2a'], '1b': ['g1', 'z2b', 'g2'], '0a': ['z3a', 'z1b', 'v', 'z3b'], '0b': ['g3', 'z1a']}


TOKENS = [('h', 0, 8), ('h', 8, 16), ('f', 0, 8), ('n', 0, 8), ('n', 8, 16), ('f', 8, 16), ('0', 0, 8), ('0', 8, 16)]


def chunks_of(half, count):
    kinds = {"h": [half], "f": range(half + 1, count), "n": range(1, half), "0": [0]}
    return [(step, lo, hi) for kind, lo, hi in TOKENS for step in kinds[kind]]


def estimate(flops=1000):
    return pl.CostEstimate(flops=flops, bytes_accessed=flops // 1000, transcendentals=0)


def in_hbm(value):
    return pltpu.with_memory_space_constraint(value, pltpu.HBM)


def contract_rows(left, right):
    return lax.dot_general(
        left, right, (((0,), (0,)), ((), ())), preferred_element_type=jnp.float32
    )


def exchange(block, axis, flip, name="p"):
    count = lax.axis_size(axis)
    with jax.named_scope(name):
        return lax.ppermute(block, axis, [(i, i ^ flip) for i in range(count)])
    return lax.ppermute(block, axis, [(i, i ^ flip) for i in range(count)])


def after(value, *earlier):
    return lax.optimization_barrier((value, *earlier))[0]


def project(laplacian, interp, pairs, jobs, *earlier, flops=1000):
    tile = interp.shape[1]
    fine_rows = interp.shape[0] // tile
    coarse_rows = fine_rows // 2
    cols = laplacian.shape[1]
    coarse_cols = cols // tile // 2
    half = lax.axis_size("row") // 2
    count = coarse_rows * tile // lax.axis_size("col")
    outs = [
        jax.ShapeDtypeStruct((count, end - begin), dtype)
        for _, _, dtype, spans in jobs
        for begin, end in spans
    ]

    def body(pairs_ref, interp_ref, lap_ref, *refs):
        out_refs = list(refs[len(earlier) : len(earlier) + len(outs)])
        lap_buf, interp_buf, whole_ref, sems = refs[len(earlier) + len(outs) :]
        row, col = lax.axis_index("row"), lax.axis_index("col")
        col_half = lax.axis_size("col") // 2
        sources = []
        for p in range(cols // tile):
            group = p // coarse_cols * col_half + col % col_half
            j = pairs_ref[col // col_half, group * coarse_cols + p % coarse_cols]
            sources.append(pl.multiple_of((j - col * 2 * coarse_cols) * tile, tile))
        copies = []
        for slot, (step, mine, _, _) in enumerate(jobs):
            owner = row if mine else row ^ half
            coarse_row = owner * coarse_rows + (col ^ step) * count // tile
            local = pairs_ref[row // half, coarse_row] - row * fine_rows
            at = pl.ds(pl.multiple_of(local * tile, tile), tile)
            for which, (ref, buf) in enumerate(((interp_ref, interp_buf), (lap_ref, lap_buf))):
                copy = pltpu.make_async_copy(ref.at[at, :], buf.at[slot], sems.at[which, slot])
                copy.start()
                copies.append(copy)
        for slot, (step, mine, _, spans) in enumerate(jobs):
            copies[2 * slot].wait()
            copies[2 * slot + 1].wait()
            left = interp_buf[slot]
            for begin, end in spans:
                out_ref = out_refs.pop(0)
                for at in range(begin, end, 2 * tile):
                    right = [
                        lap_buf[slot, :, pl.ds(source, tile)]
                        for source in sources[at // tile : at // tile + 2]
                    ]
                    result = contract_rows(left, jnp.concatenate(right, axis=1))
                    if count != tile:
                        whole_ref[...] = result
                        first = pl.multiple_of(((col ^ step) * count) % tile, count)
                        result = whole_ref[pl.ds(first, count), :]
                    out_ref[:, at - begin : at - begin + 2 * tile] = result.astype(out_ref.dtype)

    spare = (8, 128) if count == tile else (tile, 2 * tile)
    size = sum(out.size * out.dtype.itemsize for out in outs)
    size += len(jobs) * tile * (cols + tile) * 2 + spare[0] * spare[1] * 4
    return pl.pallas_call(
        body,
        out_shape=outs,
        in_specs=[pl.BlockSpec(memory_space=pltpu.SMEM)]
        + [pl.BlockSpec(memory_space=pl.ANY)] * (2 + len(earlier)),
        out_specs=[pl.BlockSpec(memory_space=pltpu.VMEM)] * len(outs),
        scratch_shapes=[
            pltpu.VMEM((len(jobs), tile, cols), jnp.bfloat16),
            pltpu.VMEM((len(jobs), tile, tile), jnp.bfloat16),
            pltpu.VMEM(spare, jnp.float32),
            pltpu.SemaphoreType.DMA((2, len(jobs))),
        ],
        compiler_params=pltpu.CompilerParams(vmem_limit_bytes=size + 4 * 1024 * 1024),
        cost_estimate=estimate(flops),
        name="project",
    )(in_hbm(pairs), in_hbm(interp), in_hbm(laplacian), *earlier)


def combine(own, begin, received, *earlier, flops=1000):
    end = begin + received.shape[1]

    def body(own_ref, received_ref, *refs):
        total = own_ref[:, begin:end].astype(jnp.float32) + received_ref[...].astype(jnp.float32)
        refs[-1][...] = total.astype(refs[-1].dtype)

    return pl.pallas_call(
        body,
        out_shape=jax.ShapeDtypeStruct(received.shape, jnp.bfloat16),
        in_specs=[pl.BlockSpec(memory_space=pltpu.VMEM)] * 2
        + [pl.BlockSpec(memory_space=pl.ANY)] * len(earlier),
        out_specs=pl.BlockSpec(memory_space=pltpu.VMEM),
        compiler_params=pltpu.CompilerParams(vmem_limit_bytes=8 * 1024 * 1024),
        cost_estimate=estimate(flops),
        name="combine",
    )(own, received, *earlier)


def gather_blocks(block, axis):
    blocks, flip = [block], lax.axis_size(axis) // 2
    while flip:
        blocks += [exchange(part, axis, flip, f"gather{flip}") for part in blocks]
        flip //= 2
    return blocks


def assemble(blocks, pairs, fine_cols, *earlier):
    rows, tile = blocks[0].shape
    fine_rows, row_count = rows // tile, lax.axis_size("row")
    coarse_cols, half = fine_cols // 2, lax.axis_size("col") // 2

    def body(pairs_ref, *refs):
        out_ref, buf, fetch = refs[-3:]
        row, col = lax.axis_index("row"), lax.axis_index("col")
        fetches = [
            pltpu.make_async_copy(ref, buf.at[pl.ds(k * rows, rows), :], fetch.at[k])
            for k, ref in enumerate(refs[: len(blocks)])
        ]
        for copy in fetches:
            copy.start()
        for copy in fetches:
            copy.wait()
        upper = col // half
        for step in range(half):
            for p in range(fine_cols):
                group = p // coarse_cols * half + (col ^ step) % half
                d = group * coarse_cols + p % coarse_cols
                for which, j in enumerate((pairs_ref[upper, d], pairs_ref[1 - upper, d])):
                    source = (j // fine_rows) ^ row
                    place, bit = 0, row_count // 2
                    while bit:
                        place = place * 2 + source % 2
                        source, bit = source // 2, bit // 2
                    at = pl.multiple_of((place * fine_rows + j % fine_rows) * tile, tile)
                    begin = ((step * fine_cols + p) * 2 + which) * tile
                    out_ref[begin : begin + tile, :] = buf[pl.ds(at, tile), :]

    return pl.pallas_call(
        body,
        out_shape=jax.ShapeDtypeStruct((len(blocks) * rows, tile), blocks[0].dtype),
        in_specs=[pl.BlockSpec(memory_space=pltpu.SMEM)]
        + [pl.BlockSpec(memory_space=pl.ANY)] * (len(blocks) + len(earlier)),
        out_specs=pl.BlockSpec(memory_space=pltpu.VMEM),
        scratch_shapes=[
            pltpu.VMEM((len(blocks) * rows, tile), blocks[0].dtype),
            pltpu.SemaphoreType.DMA((len(blocks),)),
        ],
        cost_estimate=estimate(ASSEMBLE),
        compiler_params=pltpu.CompilerParams(
            vmem_limit_bytes=len(blocks) * rows * tile * 4 + 4 * 1024 * 1024
        ),
        name="assemble",
    )(in_hbm(pairs), *blocks, *earlier)


def finish(jobs, paired_interp, before, fine_cols, *earlier):
    tile = paired_interp.shape[1]
    count = jobs[0][0][0].shape[0]
    half = lax.axis_size("col") // 2
    coarse_cols = fine_cols // 2
    width = coarse_cols * tile
    total = paired_interp.shape[0] // 2
    pieces = [part for near, far, _ in jobs for part in (*near, *far)]

    def tile_of(refs, p):
        begin = p * tile
        for ref in refs:
            if begin < ref.shape[1]:
                return ref[:, begin : begin + tile]
            begin -= ref.shape[1]

    def body(interp_ref, *refs):
        out_ref, buf, sem = refs[-3:]
        col = lax.axis_index("col")
        copies, taken = [], 0
        for n, (near, far, step) in enumerate(jobs):
            near_refs = refs[taken : taken + len(near)]
            far_refs = refs[taken + len(near) : taken + len(near) + len(far)]
            taken += len(near) + len(far)
            for part in range(2):
                for k in range(coarse_cols):
                    p = part * coarse_cols + k
                    left = jnp.concatenate([tile_of(near_refs, p), tile_of(far_refs, p)], axis=1)
                    at = (step * fine_cols + p) * 2 * tile
                    result = jnp.dot(
                        left, interp_ref[at : at + 2 * tile, :], preferred_element_type=jnp.float32
                    )
                    buf[2 * n + part, :, k * tile : (k + 1) * tile] = result.astype(buf.dtype)
                group = part * half + (col ^ step) % half
                copy = pltpu.make_async_copy(
                    buf.at[2 * n + part],
                    out_ref.at[:, pl.ds(pl.multiple_of(group * width, width), width)],
                    sem.at[2 * n + part],
                )
                copy.start()
                copies.append(copy)
        for copy in copies:
            copy.wait()

    operands = [paired_interp, *pieces]
    in_specs = [pl.BlockSpec(memory_space=pltpu.VMEM)] * len(operands)
    aliases = {}
    if before is not None:
        aliases = {len(operands): 0}
        operands.append(before)
    operands += earlier
    in_specs += [pl.BlockSpec(memory_space=pl.ANY)] * (len(operands) - len(in_specs))
    size = paired_interp.size * 2 + 2 * len(jobs) * count * (fine_cols * tile + width) * 2
    return pl.pallas_call(
        body,
        out_shape=jax.ShapeDtypeStruct((count, total), jnp.bfloat16),
        in_specs=in_specs,
        out_specs=pl.BlockSpec(memory_space=pl.ANY),
        scratch_shapes=[
            pltpu.VMEM((2 * len(jobs), count, width), jnp.bfloat16),
            pltpu.SemaphoreType.DMA((2 * len(jobs),)),
        ],
        input_output_aliases=aliases,
        cost_estimate=estimate(FINISH),
        compiler_params=pltpu.CompilerParams(vmem_limit_bytes=size + 4 * 1024 * 1024),
        name="finish",
    )(*operands)


def restrict(vectors, interp, pairs, *earlier):
    tile = interp.shape[1]
    fine_rows = interp.shape[0] // tile
    coarse_rows = fine_rows // 2
    half = lax.axis_size("row") // 2

    def body(pairs_ref, vec_ref, interp_ref, *refs):
        keep_ref, send_ref = refs[-2:]
        row = lax.axis_index("row")
        for out_ref, flip in ((keep_ref, 0), (send_ref, half)):
            for k in range(coarse_rows):
                i = pairs_ref[row // half, (row ^ flip) * coarse_rows + k] - row * fine_rows
                at = pl.ds(pl.multiple_of(i * tile, tile), tile)
                out_ref[:, k * tile : (k + 1) * tile] = jnp.dot(
                    vec_ref[:, at], interp_ref[at, :], preferred_element_type=jnp.float32
                ).astype(out_ref.dtype)

    shape = jax.ShapeDtypeStruct((vectors.shape[0], coarse_rows * tile), jnp.bfloat16)
    return pl.pallas_call(
        body,
        out_shape=(shape, shape),
        in_specs=[
            pl.BlockSpec(memory_space=pltpu.SMEM),
            pl.BlockSpec(memory_space=pltpu.VMEM),
            pl.BlockSpec(memory_space=pltpu.VMEM),
        ]
        + [pl.BlockSpec(memory_space=pl.ANY)] * len(earlier),
        out_specs=(pl.BlockSpec(memory_space=pltpu.VMEM),) * 2,
        compiler_params=pltpu.CompilerParams(vmem_limit_bytes=4 * 1024 * 1024),
        cost_estimate=estimate(),
        name="restrict",
    )(pairs, vectors, interp, *earlier)


def on_device(laplacian, interp, vectors, pairs):
    tile = interp.shape[1]
    cols = laplacian.shape[1]
    fine_rows, fine_cols = interp.shape[0] // tile, cols // tile
    row_half = lax.axis_size("row") // 2
    col_count = lax.axis_size("col")
    col_half = col_count // 2
    pairs = pairs.T

    whole = [(0, cols)]
    order = chunks_of(col_half, col_count)
    steps = list(dict.fromkeys(step for step, _, _ in order))
    spans = {
        step: [(lo * cols // 16, hi * cols // 16) for other, lo, hi in order if other == step]
        for step in steps
    }
    labels = [f"{step}{'abcdefgh'[spans[step].index((lo * cols // 16, hi * cols // 16))]}" for step, lo, hi in order]
    head = HEAD
    cut = sum(len(spans[step]) for step in steps[:head])
    sent = project(
        laplacian, interp, pairs, [(s, False, jnp.bfloat16, spans[s]) for s in steps[:head]]
    )
    sent += project(
        laplacian, interp, pairs, [(s, False, jnp.bfloat16, spans[s]) for s in steps[head:]], sent[0], flops=PFLOPS[0]
    )
    grouped = [(step, span) for step in steps for span in spans[step]]
    sent = dict(zip(grouped, sent))
    kept = project(
        laplacian, interp, pairs, [(s, True, jnp.float32, whole) for s in steps], sent[grouped[cut]], flops=PFLOPS[1]
    )
    kept = dict(zip(steps, kept))
    named, totals, held = {}, [kept[0]], {step: [] for step in steps}
    interp_blocks = keep = None
    for k, (step, lo, hi) in enumerate(order):
        name, span = labels[k], (lo * cols // 16, hi * cols // 16)
        block = sent[step, span]
        if name in YAFTER:
            block = after(block, *(named["t" + w] for w in YAFTER[name] if "t" + w in named))
        if name == ASSEMBLE_Y:
            paired_interp = assemble(interp_blocks, pairs, fine_cols)
            block = after(block, paired_interp)
        if name == VECTORS_Y:
            coarse_vectors = combine(keep, 0, far_vec, totals[-1])
            block = after(block, coarse_vectors)
        block = exchange(block, "row", row_half, "y" + name)
        waits = totals[-1:] + [named[w] for w in WAITS.get(name, ()) if w in named]
        if name == ASSEMBLE_AT:
            paired_interp = assemble(interp_blocks, pairs, fine_cols, *totals[-1:])
            waits.append(paired_interp)
        if name == VECTORS_AT:
            coarse_vectors = combine(keep, 0, far_vec, totals[-1])
            waits.append(in_hbm(coarse_vectors))
        total = combine(kept[step], span[0], block, *waits, flops=CFLOPS)
        totals.append(total)
        named["t" + name] = total
        if step:
            later = [named[w] for w in ZAFTER.get(name, ()) if w in named]
            total = exchange(after(total, *later) if later else total, "col", step, "z" + name)
        named["z" + name] = total
        held[step].append(total)
        if name == GATHER or (k + 1 == len(order) and interp_blocks is None):
            interp_blocks = gather_blocks(after(interp, totals[-1]), "row")
            for place, value in enumerate(interp_blocks):
                named[f"g{place}"] = value
        if name == VECTORS or (k + 1 == len(order) and keep is None):
            keep, send = restrict(vectors, interp, pairs, totals[-1])
            named["v"] = far_vec = exchange(send, "row", row_half, "vectors")
    if VECTORS_AT not in labels and VECTORS_Y not in labels:
        coarse_vectors = combine(keep, 0, far_vec, totals[VECDEP], flops=VECFLOPS)
    coarse = None
    if ASSEMBLE_AT not in labels and ASSEMBLE_Y not in labels:
        paired_interp = assemble(interp_blocks, pairs, fine_cols)
    jobs = [(held[step], held[step ^ col_half], step) for step in range(col_half)]
    for k in range(0, len(jobs), JOBS):
        coarse = finish(jobs[k : k + JOBS], paired_interp, coarse, fine_cols)
    return (coarse, coarse_vectors)


def solution(mesh):
    placed = (P("row", "col"), P("row", None), P(None, "row"), P())
    return jax.shard_map(
        on_device,
        mesh=mesh,
        in_specs=placed,
        out_specs=(P(("row", "col"), None), P(None, "row")),
        check_vma=False,
    )
```

```python
import jax
import jax.numpy as jnp
from jax import lax
from jax.experimental import pallas as pl
from jax.experimental.pallas import tpu as pltpu
from jax.sharding import PartitionSpec as P


YAFTER = {'3a': ['2a'], '1a': ['2b'], '1b': ['3a'], '3b': ['1a'], '0a': ['1b'], '0b': ['3b']}
HEAD = 1
CORE_PARTS = 4
GATHER = '2b'
VECTORS = '1b'
ZAFTER = {}
FINISH = 1000
PFLOPS = (1000, 1000)
CFLOPS = 1000
ASSEMBLE = 1000
WAITS = {'3a': ['z2a'], '1b': ['g1', 'z2b', 'g2'], '0a': ['z3a', 'z1b', 'v', 'z3b'], '0b': ['g3', 'z1a']}


TOKENS = [('h', 0, 8), ('h', 8, 16), ('f', 0, 8), ('n', 0, 8), ('n', 8, 16), ('f', 8, 16), ('0', 0, 8), ('0', 8, 16)]


def chunks_of(half, count):
    kinds = {"h": [half], "f": range(half + 1, count), "n": range(1, half), "0": [0]}
    return [(step, lo, hi) for kind, lo, hi in TOKENS for step in kinds[kind]]


def estimate(flops=1000):
    return pl.CostEstimate(flops=flops, bytes_accessed=flops // 1000, transcendentals=0)


def in_hbm(value):
    return pltpu.with_memory_space_constraint(value, pltpu.HBM)


def contract_rows(left, right):
    return lax.dot_general(
        left, right, (((0,), (0,)), ((), ())), preferred_element_type=jnp.float32
    )


def exchange(block, axis, flip, name="p"):
    count = lax.axis_size(axis)
    with jax.named_scope(name):
        return lax.ppermute(block, axis, [(i, i ^ flip) for i in range(count)])
    return lax.ppermute(block, axis, [(i, i ^ flip) for i in range(count)])


def after(value, *earlier):
    return lax.optimization_barrier((value, *earlier))[0]


def project(laplacian, interp, pairs, jobs, *earlier, flops=1000):
    tile = interp.shape[1]
    fine_rows = interp.shape[0] // tile
    coarse_rows = fine_rows // 2
    cols = laplacian.shape[1]
    coarse_cols = cols // tile // 2
    half = lax.axis_size("row") // 2
    count = coarse_rows * tile // lax.axis_size("col")
    outs = [
        jax.ShapeDtypeStruct((count, end - begin), dtype)
        for _, _, dtype, spans in jobs
        for begin, end in spans
    ]

    def body(pairs_ref, interp_ref, lap_ref, *refs):
        out_refs = list(refs[len(earlier) : len(earlier) + len(outs)])
        lap_buf, interp_buf, whole_ref, sems = refs[len(earlier) + len(outs) :]
        row, col = lax.axis_index("row"), lax.axis_index("col")
        col_half = lax.axis_size("col") // 2
        sources = []
        for p in range(cols // tile):
            group = p // coarse_cols * col_half + col % col_half
            j = pairs_ref[col // col_half, group * coarse_cols + p % coarse_cols]
            sources.append(pl.multiple_of((j - col * 2 * coarse_cols) * tile, tile))
        copies = []
        for slot, (step, mine, _, _) in enumerate(jobs):
            owner = row if mine else row ^ half
            coarse_row = owner * coarse_rows + (col ^ step) * count // tile
            local = pairs_ref[row // half, coarse_row] - row * fine_rows
            at = pl.ds(pl.multiple_of(local * tile, tile), tile)
            for which, (ref, buf) in enumerate(((interp_ref, interp_buf), (lap_ref, lap_buf))):
                copy = pltpu.make_async_copy(ref.at[at, :], buf.at[slot], sems.at[which, slot])
                copy.start()
                copies.append(copy)
        for slot, (step, mine, _, spans) in enumerate(jobs):
            copies[2 * slot].wait()
            copies[2 * slot + 1].wait()
            left = interp_buf[slot]
            for begin, end in spans:
                out_ref = out_refs.pop(0)
                for at in range(begin, end, 2 * tile):
                    right = [
                        lap_buf[slot, :, pl.ds(source, tile)]
                        for source in sources[at // tile : at // tile + 2]
                    ]
                    result = contract_rows(left, jnp.concatenate(right, axis=1))
                    if count != tile:
                        whole_ref[...] = result
                        first = pl.multiple_of(((col ^ step) * count) % tile, count)
                        result = whole_ref[pl.ds(first, count), :]
                    out_ref[:, at - begin : at - begin + 2 * tile] = result.astype(out_ref.dtype)

    spare = (8, 128) if count == tile else (tile, 2 * tile)
    size = sum(out.size * out.dtype.itemsize for out in outs)
    size += len(jobs) * tile * (cols + tile) * 2 + spare[0] * spare[1] * 4
    return pl.pallas_call(
        body,
        out_shape=outs,
        in_specs=[pl.BlockSpec(memory_space=pltpu.SMEM)]
        + [pl.BlockSpec(memory_space=pl.ANY)] * (2 + len(earlier)),
        out_specs=[pl.BlockSpec(memory_space=pltpu.VMEM)] * len(outs),
        scratch_shapes=[
            pltpu.VMEM((len(jobs), tile, cols), jnp.bfloat16),
            pltpu.VMEM((len(jobs), tile, tile), jnp.bfloat16),
            pltpu.VMEM(spare, jnp.float32),
            pltpu.SemaphoreType.DMA((2, len(jobs))),
        ],
        compiler_params=pltpu.CompilerParams(vmem_limit_bytes=size + 4 * 1024 * 1024),
        cost_estimate=estimate(flops),
        name="project",
    )(in_hbm(pairs), in_hbm(interp), in_hbm(laplacian), *earlier)


def combine(own, begin, received, *earlier, flops=1000):
    end = begin + received.shape[1]

    def body(own_ref, received_ref, *refs):
        total = own_ref[:, begin:end].astype(jnp.float32) + received_ref[...].astype(jnp.float32)
        refs[-1][...] = total.astype(refs[-1].dtype)

    return pl.pallas_call(
        body,
        out_shape=jax.ShapeDtypeStruct(received.shape, jnp.bfloat16),
        in_specs=[pl.BlockSpec(memory_space=pltpu.VMEM)] * 2
        + [pl.BlockSpec(memory_space=pl.ANY)] * len(earlier),
        out_specs=pl.BlockSpec(memory_space=pltpu.VMEM),
        compiler_params=pltpu.CompilerParams(vmem_limit_bytes=8 * 1024 * 1024),
        cost_estimate=estimate(flops),
        name="combine",
    )(own, received, *earlier)


def gather_blocks(block, axis):
    blocks, flip = [block], lax.axis_size(axis) // 2
    while flip > 1:
        blocks += [exchange(part, axis, flip, f"gather{flip}") for part in blocks]
        flip //= 2
    return blocks


def assemble(blocks, pairs, fine_cols, *earlier):
    rows, tile = blocks[0].shape
    fine_rows, row_count = rows // tile, lax.axis_size("row")
    coarse_rows, coarse_cols, half = fine_rows // 2, fine_cols // 2, lax.axis_size("col") // 2

    def body(pairs_ref, *refs):
        out_refs, (buf, fetch) = refs[-2 - CORE_PARTS : -2], refs[-2:]
        row, col = lax.axis_index("row"), lax.axis_index("col")
        fetches = [
            pltpu.make_async_copy(ref, buf.at[pl.ds(k * rows, rows), :], fetch.at[k])
            for k, ref in enumerate(refs[: len(blocks)])
        ]
        for copy in fetches:
            copy.start()
        for copy in fetches:
            copy.wait()
        upper, slot = col // half, 0
        for step in range(half):
            for part in range(2):
                group = part * half + (col ^ step) % half
                for first in range(0, coarse_cols, 2 * coarse_rows):
                    for k in range(coarse_rows):
                        d = group * coarse_cols + first + row % 2 * coarse_rows + k
                        for j in (pairs_ref[upper, d], pairs_ref[1 - upper, d]):
                            source = ((j // fine_rows) ^ row) // 2
                            place, bit = 0, row_count // 4
                            while bit:
                                place = place * 2 + source % 2
                                source, bit = source // 2, bit // 2
                            at = (place * fine_rows + j % fine_rows) * tile
                            out_ref, begin = out_refs[slot // length], slot % length * tile
                            out_ref[begin : begin + tile, :] = buf[
                                pl.ds(pl.multiple_of(at, tile), tile), :
                            ]
                            slot += 1

    length = half * coarse_cols * 2 // CORE_PARTS

    return pl.pallas_call(
        body,
        out_shape=[jax.ShapeDtypeStruct((length * tile, tile), blocks[0].dtype)] * CORE_PARTS,
        in_specs=[pl.BlockSpec(memory_space=pltpu.SMEM)]
        + [pl.BlockSpec(memory_space=pl.ANY)] * (len(blocks) + len(earlier)),
        out_specs=[pl.BlockSpec(memory_space=pltpu.VMEM)] * CORE_PARTS,
        scratch_shapes=[
            pltpu.VMEM((len(blocks) * rows, tile), blocks[0].dtype),
            pltpu.SemaphoreType.DMA((len(blocks),)),
        ],
        cost_estimate=estimate(ASSEMBLE),
        compiler_params=pltpu.CompilerParams(
            vmem_limit_bytes=len(blocks) * rows * tile * 4 + 4 * 1024 * 1024
        ),
        name="assemble",
    )(in_hbm(pairs), *blocks, *earlier)


def finish(jobs, paired, other_paired, own_vec, far_vec, fine_cols, fine_rows):
    part_rows, tile = paired[0].shape
    count = jobs[0][0][0].shape[0]
    half = lax.axis_size("col") // 2
    coarse_rows, coarse_cols = fine_rows // 2, fine_cols // 2
    width = coarse_cols * tile
    total = lax.axis_size("row") * fine_rows * tile // 2
    pieces = [part for near, far, _ in jobs for part in (*near, *far)]

    def tile_of(refs, p):
        begin = p * tile
        for ref in refs:
            if begin < ref.shape[1]:
                return ref[:, begin : begin + tile]
            begin -= ref.shape[1]

    def body(own_ref, far_ref, *refs):
        paired_refs, other_refs, refs = refs[:CORE_PARTS], refs[CORE_PARTS : 2 * CORE_PARTS], refs[2 * CORE_PARTS :]
        out_ref, vec_ref, buf, vec_buf, sem = refs[-5:]
        row, col = lax.axis_index("row"), lax.axis_index("col")
        vec = own_ref[...].astype(jnp.float32) + far_ref[...].astype(jnp.float32)
        vec_buf[...] = vec.astype(vec_buf.dtype)
        copies, taken, slot = [pltpu.make_async_copy(vec_buf, vec_ref, sem.at[0])], 0, 0
        copies[0].start()
        for n, (near, far, step) in enumerate(jobs):
            near_refs = refs[taken : taken + len(near)]
            far_refs = refs[taken + len(near) : taken + len(near) + len(far)]
            taken += len(near) + len(far)
            for part in range(2):
                for k in range(coarse_cols):
                    p = part * coarse_cols + k
                    left = jnp.concatenate([tile_of(near_refs, p), tile_of(far_refs, p)], axis=1)
                    place = k // (2 * coarse_rows) * coarse_rows + k % coarse_rows
                    at = (slot + place) * 2 * tile
                    which, at = at // part_rows, at % part_rows
                    right = jnp.where(
                        row % 2 == k // coarse_rows % 2,
                        paired_refs[which][at : at + 2 * tile, :],
                        other_refs[which][at : at + 2 * tile, :],
                    )
                    result = jnp.dot(left, right, preferred_element_type=jnp.float32)
                    buf[2 * n + part, :, k * tile : (k + 1) * tile] = result.astype(buf.dtype)
                slot += coarse_cols // 2
                group = part * half + (col ^ step) % half
                copy = pltpu.make_async_copy(
                    buf.at[2 * n + part],
                    out_ref.at[:, pl.ds(pl.multiple_of(group * width, width), width)],
                    sem.at[1 + 2 * n + part],
                )
                copy.start()
                copies.append(copy)
        for copy in copies:
            copy.wait()

    operands = [own_vec, far_vec, *paired, *other_paired, *pieces]
    size = CORE_PARTS * paired[0].size * 4 + 2 * len(jobs) * count * (fine_cols * tile + width) * 2
    return pl.pallas_call(
        body,
        out_shape=(
            jax.ShapeDtypeStruct((count, total), jnp.bfloat16),
            jax.ShapeDtypeStruct(own_vec.shape, jnp.bfloat16),
        ),
        in_specs=[pl.BlockSpec(memory_space=pltpu.VMEM)] * len(operands),
        out_specs=(pl.BlockSpec(memory_space=pl.ANY),) * 2,
        scratch_shapes=[
            pltpu.VMEM((2 * len(jobs), count, width), jnp.bfloat16),
            pltpu.VMEM(own_vec.shape, jnp.bfloat16),
            pltpu.SemaphoreType.DMA((1 + 2 * len(jobs),)),
        ],
        cost_estimate=estimate(FINISH),
        compiler_params=pltpu.CompilerParams(vmem_limit_bytes=size + 4 * 1024 * 1024),
        name="finish",
    )(*operands)


def restrict(vectors, interp, pairs, *earlier):
    tile = interp.shape[1]
    fine_rows = interp.shape[0] // tile
    coarse_rows = fine_rows // 2
    half = lax.axis_size("row") // 2

    def body(pairs_ref, vec_ref, interp_ref, *refs):
        keep_ref, send_ref = refs[-2:]
        row = lax.axis_index("row")
        for out_ref, flip in ((keep_ref, 0), (send_ref, half)):
            for k in range(coarse_rows):
                i = pairs_ref[row // half, (row ^ flip) * coarse_rows + k] - row * fine_rows
                at = pl.ds(pl.multiple_of(i * tile, tile), tile)
                out_ref[:, k * tile : (k + 1) * tile] = jnp.dot(
                    vec_ref[:, at], interp_ref[at, :], preferred_element_type=jnp.float32
                ).astype(out_ref.dtype)

    shape = jax.ShapeDtypeStruct((vectors.shape[0], coarse_rows * tile), jnp.bfloat16)
    return pl.pallas_call(
        body,
        out_shape=(shape, shape),
        in_specs=[
            pl.BlockSpec(memory_space=pltpu.SMEM),
            pl.BlockSpec(memory_space=pltpu.VMEM),
            pl.BlockSpec(memory_space=pltpu.VMEM),
        ]
        + [pl.BlockSpec(memory_space=pl.ANY)] * len(earlier),
        out_specs=(pl.BlockSpec(memory_space=pltpu.VMEM),) * 2,
        compiler_params=pltpu.CompilerParams(vmem_limit_bytes=4 * 1024 * 1024),
        cost_estimate=estimate(),
        name="restrict",
    )(pairs, vectors, interp, *earlier)


def on_device(laplacian, interp, vectors, pairs):
    tile = interp.shape[1]
    cols = laplacian.shape[1]
    fine_rows, fine_cols = interp.shape[0] // tile, cols // tile
    row_half = lax.axis_size("row") // 2
    col_count = lax.axis_size("col")
    col_half = col_count // 2
    pairs = pairs.T

    whole = [(0, cols)]
    order = chunks_of(col_half, col_count)
    steps = list(dict.fromkeys(step for step, _, _ in order))
    spans = {
        step: [(lo * cols // 16, hi * cols // 16) for other, lo, hi in order if other == step]
        for step in steps
    }
    labels = [f"{step}{'abcdefgh'[spans[step].index((lo * cols // 16, hi * cols // 16))]}" for step, lo, hi in order]
    head = HEAD
    cut = sum(len(spans[step]) for step in steps[:head])
    sent = project(
        laplacian, interp, pairs, [(s, False, jnp.bfloat16, spans[s]) for s in steps[:head]]
    )
    sent += project(
        laplacian, interp, pairs, [(s, False, jnp.bfloat16, spans[s]) for s in steps[head:]], sent[0], flops=PFLOPS[0]
    )
    grouped = [(step, span) for step in steps for span in spans[step]]
    sent = dict(zip(grouped, sent))
    kept = project(
        laplacian, interp, pairs, [(s, True, jnp.float32, whole) for s in steps], sent[grouped[cut]], flops=PFLOPS[1]
    )
    kept = dict(zip(steps, kept))
    named, totals, held = {}, [kept[0]], {step: [] for step in steps}
    paired = keep = None
    for k, (step, lo, hi) in enumerate(order):
        name, span = labels[k], (lo * cols // 16, hi * cols // 16)
        block = sent[step, span]
        if name in YAFTER:
            block = after(block, *(named["t" + w] for w in YAFTER[name] if "t" + w in named))
        block = exchange(block, "row", row_half, "y" + name)
        waits = totals[-1:] + [named[w] for w in WAITS.get(name, ()) if w in named]
        total = combine(kept[step], span[0], block, *waits, flops=CFLOPS)
        totals.append(total)
        named["t" + name] = total
        if step:
            later = [named[w] for w in ZAFTER.get(name, ()) if w in named]
            total = exchange(after(total, *later) if later else total, "col", step, "z" + name)
        named["z" + name] = total
        held[step].append(total)
        if name == GATHER or (k + 1 == len(order) and paired is None):
            blocks = gather_blocks(after(interp, totals[-1]), "row")
            for place, value in enumerate(blocks):
                named[f"g{place}"] = value
            paired = assemble(blocks, pairs, fine_cols)
            other_paired = [exchange(part, "row", 1, "core") for part in paired]
            for place, value in enumerate(other_paired):
                named[f"p{place}"] = value
        if name == VECTORS or (k + 1 == len(order) and keep is None):
            keep, send = restrict(vectors, interp, pairs, totals[-1])
            named["v"] = far_vec = exchange(send, "row", row_half, "vectors")
    jobs = [(held[step], held[step ^ col_half], step) for step in range(col_half)]
    return finish(jobs, paired, other_paired, keep, far_vec, fine_cols, fine_rows)


def solution(mesh):
    placed = (P("row", "col"), P("row", None), P(None, "row"), P())
    return jax.shard_map(
        on_device,
        mesh=mesh,
        in_specs=placed,
        out_specs=(P(("row", "col"), None), P(None, "row")),
        check_vma=False,
    )
```

```python
import jax
import jax.numpy as jnp
from jax import lax
from jax.experimental import pallas as pl
from jax.experimental.pallas import tpu as pltpu
from jax.sharding import PartitionSpec as P


YAFTER = {'3a': ['2a'], '1a': ['2b'], '1b': ['3a'], '3b': ['1a'], '0a': ['1b'], '0b': ['3b']}
FIRST = 2
CORE_PARTS = 4
GATHER = '2b'
VECTORS = '1b'
ZAFTER = {}
FINISH = 1000
PFLOPS = (1000, 1000)
CFLOPS = 1000
ASSEMBLE = 1000
WAITS = {'3a': ['z2a'], '1b': ['g1', 'z2b', 'g2'], '0a': ['z3a', 'z1b', 'v', 'z3b'], '0b': ['z1a', 'p0', 'p1', 'p2', 'p3']}


TOKENS = [('h', 0, 8), ('h', 8, 16), ('f', 0, 8), ('n', 0, 8), ('n', 8, 16), ('f', 8, 16), ('0', 0, 8), ('0', 8, 16)]


def chunks_of(half, count):
    kinds = {"h": [half], "f": range(half + 1, count), "n": range(1, half), "0": [0]}
    return [(step, lo, hi) for kind, lo, hi in TOKENS for step in kinds[kind]]


def estimate(flops=1000):
    return pl.CostEstimate(flops=flops, bytes_accessed=flops // 1000, transcendentals=0)


def in_hbm(value):
    return pltpu.with_memory_space_constraint(value, pltpu.HBM)


def contract_rows(left, right):
    return lax.dot_general(
        left, right, (((0,), (0,)), ((), ())), preferred_element_type=jnp.float32
    )


def exchange(block, axis, flip, name="p"):
    count = lax.axis_size(axis)
    with jax.named_scope(name):
        return lax.ppermute(block, axis, [(i, i ^ flip) for i in range(count)])
    return lax.ppermute(block, axis, [(i, i ^ flip) for i in range(count)])


def after(value, *earlier):
    return lax.optimization_barrier((value, *earlier))[0]


def project(laplacian, interp, pairs, jobs, *earlier, flops=1000):
    tile = interp.shape[1]
    fine_rows = interp.shape[0] // tile
    coarse_rows = fine_rows // 2
    cols = laplacian.shape[1]
    coarse_cols = cols // tile // 2
    half = lax.axis_size("row") // 2
    count = coarse_rows * tile // lax.axis_size("col")
    outs = [
        jax.ShapeDtypeStruct((count, end - begin), dtype)
        for _, _, dtype, spans in jobs
        for begin, end in spans
    ]

    def body(pairs_ref, interp_ref, lap_ref, *refs):
        out_refs = list(refs[len(earlier) : len(earlier) + len(outs)])
        lap_buf, interp_buf, whole_ref, sems = refs[len(earlier) + len(outs) :]
        row, col = lax.axis_index("row"), lax.axis_index("col")
        col_half = lax.axis_size("col") // 2
        sources = []
        for p in range(cols // tile):
            group = p // coarse_cols * col_half + col % col_half
            j = pairs_ref[col // col_half, group * coarse_cols + p % coarse_cols]
            sources.append(pl.multiple_of((j - col * 2 * coarse_cols) * tile, tile))
        copies = []
        for slot, (step, mine, _, _) in enumerate(jobs):
            owner = row if mine else row ^ half
            coarse_row = owner * coarse_rows + (col ^ step) * count // tile
            local = pairs_ref[row // half, coarse_row] - row * fine_rows
            at = pl.ds(pl.multiple_of(local * tile, tile), tile)
            for which, (ref, buf) in enumerate(((interp_ref, interp_buf), (lap_ref, lap_buf))):
                copy = pltpu.make_async_copy(ref.at[at, :], buf.at[slot], sems.at[which, slot])
                copy.start()
                copies.append(copy)
        for slot, (step, mine, _, spans) in enumerate(jobs):
            copies[2 * slot].wait()
            copies[2 * slot + 1].wait()
            left = interp_buf[slot]
            for begin, end in spans:
                out_ref = out_refs.pop(0)
                for at in range(begin, end, 2 * tile):
                    right = [
                        lap_buf[slot, :, pl.ds(source, tile)]
                        for source in sources[at // tile : at // tile + 2]
                    ]
                    result = contract_rows(left, jnp.concatenate(right, axis=1))
                    if count != tile:
                        whole_ref[...] = result
                        first = pl.multiple_of(((col ^ step) * count) % tile, count)
                        result = whole_ref[pl.ds(first, count), :]
                    out_ref[:, at - begin : at - begin + 2 * tile] = result.astype(out_ref.dtype)

    spare = (8, 128) if count == tile else (tile, 2 * tile)
    size = sum(out.size * out.dtype.itemsize for out in outs)
    size += len(jobs) * tile * (cols + tile) * 2 + spare[0] * spare[1] * 4
    return pl.pallas_call(
        body,
        out_shape=outs,
        in_specs=[pl.BlockSpec(memory_space=pltpu.SMEM)]
        + [pl.BlockSpec(memory_space=pl.ANY)] * (2 + len(earlier)),
        out_specs=[pl.BlockSpec(memory_space=pltpu.VMEM)] * len(outs),
        scratch_shapes=[
            pltpu.VMEM((len(jobs), tile, cols), jnp.bfloat16),
            pltpu.VMEM((len(jobs), tile, tile), jnp.bfloat16),
            pltpu.VMEM(spare, jnp.float32),
            pltpu.SemaphoreType.DMA((2, len(jobs))),
        ],
        compiler_params=pltpu.CompilerParams(vmem_limit_bytes=size + 4 * 1024 * 1024),
        cost_estimate=estimate(flops),
        name="project",
    )(in_hbm(pairs), in_hbm(interp), in_hbm(laplacian), *earlier)


def combine(own, begin, received, *earlier, flops=1000):
    end = begin + received.shape[1]

    def body(own_ref, received_ref, *refs):
        total = own_ref[:, begin:end].astype(jnp.float32) + received_ref[...].astype(jnp.float32)
        refs[-1][...] = total.astype(refs[-1].dtype)

    return pl.pallas_call(
        body,
        out_shape=jax.ShapeDtypeStruct(received.shape, jnp.bfloat16),
        in_specs=[pl.BlockSpec(memory_space=pltpu.VMEM)] * 2
        + [pl.BlockSpec(memory_space=pl.ANY)] * len(earlier),
        out_specs=pl.BlockSpec(memory_space=pltpu.VMEM),
        compiler_params=pltpu.CompilerParams(vmem_limit_bytes=8 * 1024 * 1024),
        cost_estimate=estimate(flops),
        name="combine",
    )(own, received, *earlier)


def gather_blocks(block, axis):
    blocks, flip = [block], lax.axis_size(axis) // 2
    while flip > 1:
        blocks += [exchange(part, axis, flip, f"gather{flip}") for part in blocks]
        flip //= 2
    return blocks


def assemble(blocks, pairs, fine_cols, *earlier):
    rows, tile = blocks[0].shape
    fine_rows, row_count = rows // tile, lax.axis_size("row")
    coarse_rows, coarse_cols, half = fine_rows // 2, fine_cols // 2, lax.axis_size("col") // 2

    def body(pairs_ref, *refs):
        out_refs, (buf, fetch) = refs[-2 - CORE_PARTS : -2], refs[-2:]
        row, col = lax.axis_index("row"), lax.axis_index("col")
        fetches = [
            pltpu.make_async_copy(ref, buf.at[pl.ds(k * rows, rows), :], fetch.at[k])
            for k, ref in enumerate(refs[: len(blocks)])
        ]
        for copy in fetches:
            copy.start()
        for copy in fetches:
            copy.wait()
        upper, slot = col // half, 0
        for step in range(half):
            for part in range(2):
                group = part * half + (col ^ step) % half
                for first in range(0, coarse_cols, 2 * coarse_rows):
                    for k in range(coarse_rows):
                        d = group * coarse_cols + first + row % 2 * coarse_rows + k
                        for j in (pairs_ref[upper, d], pairs_ref[1 - upper, d]):
                            source = ((j // fine_rows) ^ row) // 2
                            place, bit = 0, row_count // 4
                            while bit:
                                place = place * 2 + source % 2
                                source, bit = source // 2, bit // 2
                            at = (place * fine_rows + j % fine_rows) * tile
                            out_ref, begin = out_refs[slot // length], slot % length * tile
                            out_ref[begin : begin + tile, :] = buf[
                                pl.ds(pl.multiple_of(at, tile), tile), :
                            ]
                            slot += 1

    length = half * coarse_cols * 2 // CORE_PARTS

    return pl.pallas_call(
        body,
        out_shape=[jax.ShapeDtypeStruct((length * tile, tile), blocks[0].dtype)] * CORE_PARTS,
        in_specs=[pl.BlockSpec(memory_space=pltpu.SMEM)]
        + [pl.BlockSpec(memory_space=pl.ANY)] * (len(blocks) + len(earlier)),
        out_specs=[pl.BlockSpec(memory_space=pltpu.VMEM)] * CORE_PARTS,
        scratch_shapes=[
            pltpu.VMEM((len(blocks) * rows, tile), blocks[0].dtype),
            pltpu.SemaphoreType.DMA((len(blocks),)),
        ],
        cost_estimate=estimate(ASSEMBLE),
        compiler_params=pltpu.CompilerParams(
            vmem_limit_bytes=len(blocks) * rows * tile * 4 + 4 * 1024 * 1024
        ),
        name="assemble",
    )(in_hbm(pairs), *blocks, *earlier)


def finish(jobs, paired, other_paired, own_vec, far_vec, fine_cols, fine_rows):
    part_rows, tile = paired[0].shape
    count = jobs[0][0][0].shape[0]
    half = lax.axis_size("col") // 2
    coarse_rows, coarse_cols = fine_rows // 2, fine_cols // 2
    width = coarse_cols * tile
    total = lax.axis_size("row") * fine_rows * tile // 2
    pieces = [part for near, far, _ in jobs for part in (*near, *far)]

    def tile_of(refs, p):
        begin = p * tile
        for ref in refs:
            if begin < ref.shape[1]:
                return ref[:, begin : begin + tile]
            begin -= ref.shape[1]

    def body(own_ref, far_ref, *refs):
        paired_refs, other_refs, refs = refs[:CORE_PARTS], refs[CORE_PARTS : 2 * CORE_PARTS], refs[2 * CORE_PARTS :]
        out_ref, vec_ref, buf, vec_buf, sem = refs[-5:]
        row, col = lax.axis_index("row"), lax.axis_index("col")
        vec = own_ref[...].astype(jnp.float32) + far_ref[...].astype(jnp.float32)
        vec_buf[...] = vec.astype(vec_buf.dtype)
        copies, taken, slot = [pltpu.make_async_copy(vec_buf, vec_ref, sem.at[0])], 0, 0
        copies[0].start()
        for n, (near, far, step) in enumerate(jobs):
            near_refs = refs[taken : taken + len(near)]
            far_refs = refs[taken + len(near) : taken + len(near) + len(far)]
            taken += len(near) + len(far)
            for part in range(2):
                for k in range(coarse_cols):
                    p = part * coarse_cols + k
                    left = jnp.concatenate([tile_of(near_refs, p), tile_of(far_refs, p)], axis=1)
                    place = k // (2 * coarse_rows) * coarse_rows + k % coarse_rows
                    at = (slot + place) * 2 * tile
                    which, at = at // part_rows, at % part_rows
                    right = jnp.where(
                        row % 2 == k // coarse_rows % 2,
                        paired_refs[which][at : at + 2 * tile, :],
                        other_refs[which][at : at + 2 * tile, :],
                    )
                    result = jnp.dot(left, right, preferred_element_type=jnp.float32)
                    buf[2 * n + part, :, k * tile : (k + 1) * tile] = result.astype(buf.dtype)
                slot += coarse_cols // 2
                group = part * half + (col ^ step) % half
                copy = pltpu.make_async_copy(
                    buf.at[2 * n + part],
                    out_ref.at[:, pl.ds(pl.multiple_of(group * width, width), width)],
                    sem.at[1 + 2 * n + part],
                )
                copy.start()
                copies.append(copy)
        for copy in copies:
            copy.wait()

    operands = [own_vec, far_vec, *paired, *other_paired, *pieces]
    size = CORE_PARTS * paired[0].size * 4 + 2 * len(jobs) * count * (fine_cols * tile + width) * 2
    return pl.pallas_call(
        body,
        out_shape=(
            jax.ShapeDtypeStruct((count, total), jnp.bfloat16),
            jax.ShapeDtypeStruct(own_vec.shape, jnp.bfloat16),
        ),
        in_specs=[pl.BlockSpec(memory_space=pltpu.VMEM)] * len(operands),
        out_specs=(pl.BlockSpec(memory_space=pl.ANY),) * 2,
        scratch_shapes=[
            pltpu.VMEM((2 * len(jobs), count, width), jnp.bfloat16),
            pltpu.VMEM(own_vec.shape, jnp.bfloat16),
            pltpu.SemaphoreType.DMA((1 + 2 * len(jobs),)),
        ],
        cost_estimate=estimate(FINISH),
        compiler_params=pltpu.CompilerParams(vmem_limit_bytes=size + 4 * 1024 * 1024),
        name="finish",
    )(*operands)


def restrict(vectors, interp, pairs, *earlier):
    tile = interp.shape[1]
    fine_rows = interp.shape[0] // tile
    coarse_rows = fine_rows // 2
    half = lax.axis_size("row") // 2

    def body(pairs_ref, vec_ref, interp_ref, *refs):
        keep_ref, send_ref = refs[-2:]
        row = lax.axis_index("row")
        for out_ref, flip in ((keep_ref, 0), (send_ref, half)):
            for k in range(coarse_rows):
                i = pairs_ref[row // half, (row ^ flip) * coarse_rows + k] - row * fine_rows
                at = pl.ds(pl.multiple_of(i * tile, tile), tile)
                out_ref[:, k * tile : (k + 1) * tile] = jnp.dot(
                    vec_ref[:, at], interp_ref[at, :], preferred_element_type=jnp.float32
                ).astype(out_ref.dtype)

    shape = jax.ShapeDtypeStruct((vectors.shape[0], coarse_rows * tile), jnp.bfloat16)
    return pl.pallas_call(
        body,
        out_shape=(shape, shape),
        in_specs=[
            pl.BlockSpec(memory_space=pltpu.SMEM),
            pl.BlockSpec(memory_space=pltpu.VMEM),
            pl.BlockSpec(memory_space=pltpu.VMEM),
        ]
        + [pl.BlockSpec(memory_space=pl.ANY)] * len(earlier),
        out_specs=(pl.BlockSpec(memory_space=pltpu.VMEM),) * 2,
        compiler_params=pltpu.CompilerParams(vmem_limit_bytes=4 * 1024 * 1024),
        cost_estimate=estimate(),
        name="restrict",
    )(pairs, vectors, interp, *earlier)


def on_device(laplacian, interp, vectors, pairs):
    tile = interp.shape[1]
    cols = laplacian.shape[1]
    fine_rows, fine_cols = interp.shape[0] // tile, cols // tile
    row_half = lax.axis_size("row") // 2
    col_count = lax.axis_size("col")
    col_half = col_count // 2
    pairs = pairs.T

    whole = [(0, cols)]
    order = chunks_of(col_half, col_count)
    steps = list(dict.fromkeys(step for step, _, _ in order))
    spans = {
        step: [(lo * cols // 16, hi * cols // 16) for other, lo, hi in order if other == step]
        for step in steps
    }
    labels = [f"{step}{'abcdefgh'[spans[step].index((lo * cols // 16, hi * cols // 16))]}" for step, lo, hi in order]
    first, rest = steps[0], steps[1:]
    cut = len(spans[first])
    sent = project(laplacian, interp, pairs, [(first, False, jnp.bfloat16, spans[first][:FIRST])])
    jobs = [(first, False, jnp.bfloat16, spans[first][FIRST:])] if FIRST < cut else []
    jobs += [(s, False, jnp.bfloat16, spans[s]) for s in rest]
    sent += project(laplacian, interp, pairs, jobs, sent[0], flops=PFLOPS[0])
    grouped = [(step, span) for step in steps for span in spans[step]]
    sent = dict(zip(grouped, sent))
    kept = project(
        laplacian, interp, pairs, [(s, True, jnp.float32, whole) for s in steps], sent[grouped[cut]], flops=PFLOPS[1]
    )
    kept = dict(zip(steps, kept))
    named, totals, held = {}, [kept[0]], {step: [] for step in steps}
    paired = keep = None
    for k, (step, lo, hi) in enumerate(order):
        name, span = labels[k], (lo * cols // 16, hi * cols // 16)
        block = sent[step, span]
        if name in YAFTER:
            block = after(block, *(named["t" + w] for w in YAFTER[name] if "t" + w in named))
        block = exchange(block, "row", row_half, "y" + name)
        waits = totals[-1:] + [named[w] for w in WAITS.get(name, ()) if w in named]
        total = combine(kept[step], span[0], block, *waits, flops=CFLOPS)
        totals.append(total)
        named["t" + name] = total
        if step:
            later = [named[w] for w in ZAFTER.get(name, ()) if w in named]
            total = exchange(after(total, *later) if later else total, "col", step, "z" + name)
        named["z" + name] = total
        held[step].append(total)
        if name == GATHER or (k + 1 == len(order) and paired is None):
            blocks = gather_blocks(after(interp, totals[-1]), "row")
            for place, value in enumerate(blocks):
                named[f"g{place}"] = value
            paired = assemble(blocks, pairs, fine_cols)
            other_paired = [exchange(part, "row", 1, "core") for part in paired]
            for place, value in enumerate(other_paired):
                named[f"p{place}"] = value
        if name == VECTORS or (k + 1 == len(order) and keep is None):
            keep, send = restrict(vectors, interp, pairs, totals[-1])
            named["v"] = far_vec = exchange(send, "row", row_half, "vectors")
    jobs = [(held[step], held[step ^ col_half], step) for step in range(col_half)]
    return finish(jobs, paired, other_paired, keep, far_vec, fine_cols, fine_rows)


def solution(mesh):
    placed = (P("row", "col"), P("row", None), P(None, "row"), P())
    return jax.shard_map(
        on_device,
        mesh=mesh,
        in_specs=placed,
        out_specs=(P(("row", "col"), None), P(None, "row")),
        check_vma=False,
    )
```

```python
import jax
import jax.numpy as jnp
from jax import lax
from jax.experimental import pallas as pl
from jax.experimental.pallas import tpu as pltpu
from jax.sharding import PartitionSpec as P


CHUNKS = [
    ("h", 0, 8),
    ("h", 8, 16),
    ("f", 0, 8),
    ("n", 0, 8),
    ("n", 8, 16),
    ("f", 8, 16),
    ("0", 0, 8),
    ("0", 8, 16),
]
ROW_AFTER = {"3a": "2a", "1a": "2b", "1b": "3a", "3b": "1a", "0a": "1b", "0b": "3b"}
WAITS = {
    "3a": ["z2a"],
    "1b": ["z2b", "g2"],
    "0a": ["z3a", "z1b", "v", "z3b"],
    "0b": ["z1a", "p1", "p2", "p3"],
}
GATHER, VECTORS = "2b", "1b"
CORE_PARTS = 4


def chunks_of(half, count):
    kinds = {"h": [half], "f": range(half + 1, count), "n": range(1, half), "0": [0]}
    return [(step, lo, hi) for kind, lo, hi in CHUNKS for step in kinds[kind]]


ESTIMATE = pl.CostEstimate(flops=1000, bytes_accessed=1, transcendentals=0)


def in_hbm(value):
    return pltpu.with_memory_space_constraint(value, pltpu.HBM)


def contract_rows(left, right):
    return lax.dot_general(
        left, right, (((0,), (0,)), ((), ())), preferred_element_type=jnp.float32
    )


def exchange(block, axis, flip, name):
    count = lax.axis_size(axis)
    with jax.named_scope(name):
        return lax.ppermute(block, axis, [(i, i ^ flip) for i in range(count)])


def after(value, *earlier):
    return lax.optimization_barrier((value, *earlier))[0]


def project(laplacian, interp, pairs, jobs, *earlier):
    tile = interp.shape[1]
    fine_rows = interp.shape[0] // tile
    coarse_rows = fine_rows // 2
    cols = laplacian.shape[1]
    coarse_cols = cols // tile // 2
    half = lax.axis_size("row") // 2
    count = coarse_rows * tile // lax.axis_size("col")
    outs = [
        jax.ShapeDtypeStruct((count, end - begin), dtype)
        for _, _, dtype, spans in jobs
        for begin, end in spans
    ]

    def body(pairs_ref, interp_ref, lap_ref, *refs):
        out_refs = list(refs[len(earlier) : len(earlier) + len(outs)])
        lap_buf, interp_buf, whole_ref, sems = refs[len(earlier) + len(outs) :]
        row, col = lax.axis_index("row"), lax.axis_index("col")
        col_half = lax.axis_size("col") // 2
        sources = []
        for p in range(cols // tile):
            group = p // coarse_cols * col_half + col % col_half
            j = pairs_ref[col // col_half, group * coarse_cols + p % coarse_cols]
            sources.append(pl.multiple_of((j - col * 2 * coarse_cols) * tile, tile))
        copies = []
        for slot, (step, mine, _, _) in enumerate(jobs):
            owner = row if mine else row ^ half
            coarse_row = owner * coarse_rows + (col ^ step) * count // tile
            local = pairs_ref[row // half, coarse_row] - row * fine_rows
            at = pl.ds(pl.multiple_of(local * tile, tile), tile)
            for which, (ref, buf) in enumerate(((interp_ref, interp_buf), (lap_ref, lap_buf))):
                copy = pltpu.make_async_copy(ref.at[at, :], buf.at[slot], sems.at[which, slot])
                copy.start()
                copies.append(copy)
        for slot, (step, mine, _, spans) in enumerate(jobs):
            copies[2 * slot].wait()
            copies[2 * slot + 1].wait()
            left = interp_buf[slot]
            for begin, end in spans:
                out_ref = out_refs.pop(0)
                for at in range(begin, end, 2 * tile):
                    right = [
                        lap_buf[slot, :, pl.ds(source, tile)]
                        for source in sources[at // tile : at // tile + 2]
                    ]
                    result = contract_rows(left, jnp.concatenate(right, axis=1))
                    if count != tile:
                        whole_ref[...] = result
                        first = pl.multiple_of(((col ^ step) * count) % tile, count)
                        result = whole_ref[pl.ds(first, count), :]
                    out_ref[:, at - begin : at - begin + 2 * tile] = result.astype(out_ref.dtype)

    spare = (8, 128) if count == tile else (tile, 2 * tile)
    size = sum(out.size * out.dtype.itemsize for out in outs)
    size += len(jobs) * tile * (cols + tile) * 2 + spare[0] * spare[1] * 4
    return pl.pallas_call(
        body,
        out_shape=outs,
        in_specs=[pl.BlockSpec(memory_space=pltpu.SMEM)]
        + [pl.BlockSpec(memory_space=pl.ANY)] * (2 + len(earlier)),
        out_specs=[pl.BlockSpec(memory_space=pltpu.VMEM)] * len(outs),
        scratch_shapes=[
            pltpu.VMEM((len(jobs), tile, cols), jnp.bfloat16),
            pltpu.VMEM((len(jobs), tile, tile), jnp.bfloat16),
            pltpu.VMEM(spare, jnp.float32),
            pltpu.SemaphoreType.DMA((2, len(jobs))),
        ],
        compiler_params=pltpu.CompilerParams(vmem_limit_bytes=size + 4 * 1024 * 1024),
        cost_estimate=ESTIMATE,
        name="project",
    )(in_hbm(pairs), in_hbm(interp), in_hbm(laplacian), *earlier)


def combine(own, begin, received, *earlier):
    end = begin + received.shape[1]

    def body(own_ref, received_ref, *refs):
        total = own_ref[:, begin:end].astype(jnp.float32) + received_ref[...].astype(jnp.float32)
        refs[-1][...] = total.astype(refs[-1].dtype)

    return pl.pallas_call(
        body,
        out_shape=jax.ShapeDtypeStruct(received.shape, jnp.bfloat16),
        in_specs=[pl.BlockSpec(memory_space=pltpu.VMEM)] * 2
        + [pl.BlockSpec(memory_space=pl.ANY)] * len(earlier),
        out_specs=pl.BlockSpec(memory_space=pltpu.VMEM),
        compiler_params=pltpu.CompilerParams(vmem_limit_bytes=8 * 1024 * 1024),
        cost_estimate=ESTIMATE,
        name="combine",
    )(own, received, *earlier)


def gather_blocks(block, axis):
    blocks, flip = [block], lax.axis_size(axis) // 2
    while flip > 1:
        blocks += [exchange(part, axis, flip, f"gather{flip}") for part in blocks]
        flip //= 2
    return blocks


def assemble(blocks, pairs, fine_cols, *earlier):
    rows, tile = blocks[0].shape
    fine_rows, row_count = rows // tile, lax.axis_size("row")
    coarse_rows, coarse_cols, half = fine_rows // 2, fine_cols // 2, lax.axis_size("col") // 2

    def body(pairs_ref, *refs):
        out_refs, (buf, fetch) = refs[-2 - CORE_PARTS : -2], refs[-2:]
        row, col = lax.axis_index("row"), lax.axis_index("col")
        fetches = [
            pltpu.make_async_copy(ref, buf.at[pl.ds(k * rows, rows), :], fetch.at[k])
            for k, ref in enumerate(refs[: len(blocks)])
        ]
        for copy in fetches:
            copy.start()
        for copy in fetches:
            copy.wait()
        upper, slot = col // half, 0
        for step in range(half):
            for part in range(2):
                group = part * half + (col ^ step) % half
                for first in range(0, coarse_cols, 2 * coarse_rows):
                    for k in range(coarse_rows):
                        d = group * coarse_cols + first + row % 2 * coarse_rows + k
                        for j in (pairs_ref[upper, d], pairs_ref[1 - upper, d]):
                            source = ((j // fine_rows) ^ row) // 2
                            place, bit = 0, row_count // 4
                            while bit:
                                place = place * 2 + source % 2
                                source, bit = source // 2, bit // 2
                            at = (place * fine_rows + j % fine_rows) * tile
                            out_ref, begin = out_refs[slot // length], slot % length * tile
                            out_ref[begin : begin + tile, :] = buf[
                                pl.ds(pl.multiple_of(at, tile), tile), :
                            ]
                            slot += 1

    length = half * coarse_cols * 2 // CORE_PARTS

    return pl.pallas_call(
        body,
        out_shape=[jax.ShapeDtypeStruct((length * tile, tile), blocks[0].dtype)] * CORE_PARTS,
        in_specs=[pl.BlockSpec(memory_space=pltpu.SMEM)]
        + [pl.BlockSpec(memory_space=pl.ANY)] * (len(blocks) + len(earlier)),
        out_specs=[pl.BlockSpec(memory_space=pltpu.VMEM)] * CORE_PARTS,
        scratch_shapes=[
            pltpu.VMEM((len(blocks) * rows, tile), blocks[0].dtype),
            pltpu.SemaphoreType.DMA((len(blocks),)),
        ],
        cost_estimate=ESTIMATE,
        compiler_params=pltpu.CompilerParams(
            vmem_limit_bytes=len(blocks) * rows * tile * 4 + 4 * 1024 * 1024
        ),
        name="assemble",
    )(in_hbm(pairs), *blocks, *earlier)


def finish(jobs, paired, other_paired, own_vec, far_vec, fine_cols, fine_rows):
    part_rows, tile = paired[0].shape
    count = jobs[0][0][0].shape[0]
    half = lax.axis_size("col") // 2
    coarse_rows, coarse_cols = fine_rows // 2, fine_cols // 2
    width = coarse_cols * tile
    total = lax.axis_size("row") * fine_rows * tile // 2
    pieces = [part for near, far, _ in jobs for part in (*near, *far)]

    def tile_of(refs, p):
        begin = p * tile
        for ref in refs:
            if begin < ref.shape[1]:
                return ref[:, begin : begin + tile]
            begin -= ref.shape[1]

    def body(own_ref, far_ref, *refs):
        paired_refs, other_refs = refs[:CORE_PARTS], refs[CORE_PARTS : 2 * CORE_PARTS]
        refs = refs[2 * CORE_PARTS :]
        out_ref, vec_ref, buf, vec_buf, sem = refs[-5:]
        row, col = lax.axis_index("row"), lax.axis_index("col")
        vec = own_ref[...].astype(jnp.float32) + far_ref[...].astype(jnp.float32)
        vec_buf[...] = vec.astype(vec_buf.dtype)
        copies, taken, slot = [pltpu.make_async_copy(vec_buf, vec_ref, sem.at[0])], 0, 0
        copies[0].start()
        for n, (near, far, step) in enumerate(jobs):
            near_refs = refs[taken : taken + len(near)]
            far_refs = refs[taken + len(near) : taken + len(near) + len(far)]
            taken += len(near) + len(far)
            for part in range(2):
                for k in range(coarse_cols):
                    p = part * coarse_cols + k
                    left = jnp.concatenate([tile_of(near_refs, p), tile_of(far_refs, p)], axis=1)
                    place = k // (2 * coarse_rows) * coarse_rows + k % coarse_rows
                    at = (slot + place) * 2 * tile
                    which, at = at // part_rows, at % part_rows
                    right = jnp.where(
                        row % 2 == k // coarse_rows % 2,
                        paired_refs[which][at : at + 2 * tile, :],
                        other_refs[which][at : at + 2 * tile, :],
                    )
                    result = jnp.dot(left, right, preferred_element_type=jnp.float32)
                    buf[2 * n + part, :, k * tile : (k + 1) * tile] = result.astype(buf.dtype)
                slot += coarse_cols // 2
                group = part * half + (col ^ step) % half
                copy = pltpu.make_async_copy(
                    buf.at[2 * n + part],
                    out_ref.at[:, pl.ds(pl.multiple_of(group * width, width), width)],
                    sem.at[1 + 2 * n + part],
                )
                copy.start()
                copies.append(copy)
        for copy in copies:
            copy.wait()

    operands = [own_vec, far_vec, *paired, *other_paired, *pieces]
    size = CORE_PARTS * paired[0].size * 4 + 2 * len(jobs) * count * (fine_cols * tile + width) * 2
    return pl.pallas_call(
        body,
        out_shape=(
            jax.ShapeDtypeStruct((count, total), jnp.bfloat16),
            jax.ShapeDtypeStruct(own_vec.shape, jnp.bfloat16),
        ),
        in_specs=[pl.BlockSpec(memory_space=pltpu.VMEM)] * len(operands),
        out_specs=(pl.BlockSpec(memory_space=pl.ANY),) * 2,
        scratch_shapes=[
            pltpu.VMEM((2 * len(jobs), count, width), jnp.bfloat16),
            pltpu.VMEM(own_vec.shape, jnp.bfloat16),
            pltpu.SemaphoreType.DMA((1 + 2 * len(jobs),)),
        ],
        cost_estimate=ESTIMATE,
        compiler_params=pltpu.CompilerParams(vmem_limit_bytes=size + 4 * 1024 * 1024),
        name="finish",
    )(*operands)


def restrict(vectors, interp, pairs, *earlier):
    tile = interp.shape[1]
    fine_rows = interp.shape[0] // tile
    coarse_rows = fine_rows // 2
    half = lax.axis_size("row") // 2

    def body(pairs_ref, vec_ref, interp_ref, *refs):
        keep_ref, send_ref = refs[-2:]
        row = lax.axis_index("row")
        for out_ref, flip in ((keep_ref, 0), (send_ref, half)):
            for k in range(coarse_rows):
                i = pairs_ref[row // half, (row ^ flip) * coarse_rows + k] - row * fine_rows
                at = pl.ds(pl.multiple_of(i * tile, tile), tile)
                out_ref[:, k * tile : (k + 1) * tile] = jnp.dot(
                    vec_ref[:, at], interp_ref[at, :], preferred_element_type=jnp.float32
                ).astype(out_ref.dtype)

    shape = jax.ShapeDtypeStruct((vectors.shape[0], coarse_rows * tile), jnp.bfloat16)
    return pl.pallas_call(
        body,
        out_shape=(shape, shape),
        in_specs=[
            pl.BlockSpec(memory_space=pltpu.SMEM),
            pl.BlockSpec(memory_space=pltpu.VMEM),
            pl.BlockSpec(memory_space=pltpu.VMEM),
        ]
        + [pl.BlockSpec(memory_space=pl.ANY)] * len(earlier),
        out_specs=(pl.BlockSpec(memory_space=pltpu.VMEM),) * 2,
        compiler_params=pltpu.CompilerParams(vmem_limit_bytes=4 * 1024 * 1024),
        cost_estimate=ESTIMATE,
        name="restrict",
    )(pairs, vectors, interp, *earlier)


def on_device(laplacian, interp, vectors, pairs):
    tile = interp.shape[1]
    cols = laplacian.shape[1]
    fine_rows, fine_cols = interp.shape[0] // tile, cols // tile
    row_half = lax.axis_size("row") // 2
    col_count = lax.axis_size("col")
    col_half = col_count // 2
    pairs = pairs.T

    whole = [(0, cols)]
    order = chunks_of(col_half, col_count)
    steps = list(dict.fromkeys(step for step, _, _ in order))
    spans = {
        step: [(lo * cols // 16, hi * cols // 16) for other, lo, hi in order if other == step]
        for step in steps
    }
    first, rest = steps[0], steps[1:]
    cut = len(spans[first])
    sent = project(laplacian, interp, pairs, [(first, False, jnp.bfloat16, spans[first])])
    jobs = [(s, False, jnp.bfloat16, spans[s]) for s in rest]
    sent += project(laplacian, interp, pairs, jobs, sent[0])
    grouped = [(step, span) for step in steps for span in spans[step]]
    sent = dict(zip(grouped, sent))
    kept = project(
        laplacian, interp, pairs, [(s, True, jnp.float32, whole) for s in steps], sent[grouped[cut]]
    )
    kept = dict(zip(steps, kept))
    named, totals, held = {}, [kept[0]], {step: [] for step in steps}
    paired = keep = None
    for k, (step, lo, hi) in enumerate(order):
        span = (lo * cols // 16, hi * cols // 16)
        name = f"{step}{'abcdefgh'[spans[step].index(span)]}"
        block = sent[step, span]
        if "t" + ROW_AFTER.get(name, "") in named:
            block = after(block, named["t" + ROW_AFTER[name]])
        block = exchange(block, "row", row_half, "y" + name)
        waits = totals[-1:] + [named[w] for w in WAITS.get(name, ()) if w in named]
        total = combine(kept[step], span[0], block, *waits)
        totals.append(total)
        named["t" + name] = total
        if step:
            total = exchange(total, "col", step, "z" + name)
        named["z" + name] = total
        held[step].append(total)
        if name == GATHER or (k + 1 == len(order) and paired is None):
            blocks = gather_blocks(after(interp, totals[-1]), "row")
            for place, value in enumerate(blocks):
                named[f"g{place}"] = value
            paired = assemble(blocks, pairs, fine_cols)
            other_paired = [exchange(part, "row", 1, "core") for part in paired]
            for place, value in enumerate(other_paired):
                named[f"p{place}"] = value
        if name == VECTORS or (k + 1 == len(order) and keep is None):
            keep, send = restrict(vectors, interp, pairs, totals[-1])
            named["v"] = far_vec = exchange(send, "row", row_half, "vectors")
    jobs = [(held[step], held[step ^ col_half], step) for step in range(col_half)]
    return finish(jobs, paired, other_paired, keep, far_vec, fine_cols, fine_rows)


def solution(mesh):
    placed = (P("row", "col"), P("row", None), P(None, "row"), P())
    return jax.shard_map(
        on_device,
        mesh=mesh,
        in_specs=placed,
        out_specs=(P(("row", "col"), None), P(None, "row")),
        check_vma=False,
    )
```
